256 devices in a mesh: lat: 8 (over x_lo, y), lon: 32 (over x_hi, z, core).
Axes of the slice: x: 4 (x_hi: 2, x_lo: 2; x = x_hi * 2 + x_lo), y: 4, z: 8, core: 2. Of those that a mesh axis runs over, the one named last changes fastest.
Arguments:
- field: bfloat16 [2, 144, 768, 512], P(None, 'lat', 'lon'), may hold values from -6 to 6
- weights: bfloat16 [2, 512, 6144], P(None, 'lon'), may hold values from -4 to 4
- gains: float32 [2, 2, 512], replicated, may hold values from 0.1 to 1.9
Outputs:
- result: bfloat16 [2, 144, 768, 512], P(None, 'lat', 'lon')
The draws below stay inside these ranges and needn't reach their ends.
All inputs are finite; a program needn't handle non-finite values.
Results may differ from the reference program's by a relative error of at most 0.012.
Values may be sent and summed in bfloat16 or wider, within the bound.
A program may use at most 128 MiB of HBM per device.

```python
import jax
import jax.numpy as jnp
from jax import lax

D = 512
HEAD = 64
FF = 2048
LEVELS = 2
WIN_H = 6
WIN_W = 12
SHIFT_H = 3
SHIFT_W = 6
NH = 144
NW = 768


def draw_weights(key, part):
    key = jax.random.fold_in(key, 7)
    base_key = jax.random.fold_in(key, 0)
    total = 4 * D + 2 * FF
    base = jax.random.normal(base_key, (2, D, total), jnp.float32)
    columns = jnp.arange(total)
    scale = jnp.where(columns < 4 * D + FF, D ** (-0.5), FF ** (-0.5)).astype(jnp.float32)
    matrix = base * scale
    return matrix.astype(jnp.bfloat16)


def level_of(rng, extent, shards, least, top_value):
    level = 1.0
    for axis_at, parts in shards:
        steps = jax.random.uniform(jax.random.fold_in(jax.random.fold_in(rng, 6), axis_at), (parts,), jnp.float32, least / len(shards), top_value / len(shards))
        level = level * jnp.repeat(jnp.exp(steps), extent[axis_at] // parts).reshape((-1,) + (1,) * (len(extent) - 1 - axis_at))
    return level


def normal_values(own_key, shape, deviation, reach, pieces=(), kind=jnp.bfloat16):
    loudness = level_of(own_key, shape, pieces, -0.22, 0.18) if pieces else 1.0
    array = jax.random.normal(own_key, shape, jnp.float32) * deviation * loudness
    return jnp.minimum(jnp.maximum(array, -reach), reach).astype(kind)


def setup_inputs(seed: int = 0) -> dict:
    seeds = jax.random.split(jax.random.key(seed), 4)
    field = normal_values(seeds[0], (LEVELS, NH, NW, D), 1.0, 6.0, ((1, 8), (2, 32)))
    weights = draw_weights(jax.random.fold_in(seeds[3], 71), 0)
    gains = jnp.clip(1.0 + 0.18 * jax.random.normal(seeds[2], (2, 2, D), jnp.float32), 0.1, 1.9)
    return dict(field=field, weights=weights, gains=gains)


def layer_norm(values, gain):
    values = values.astype(jnp.float32)
    center = values - lax.optimization_barrier(jnp.mean(values, axis=-1, keepdims=True))
    spread = lax.optimization_barrier(jnp.mean(center * center, axis=-1, keepdims=True))
    return center * lax.rsqrt(spread + 1e-05) * gain

def window_layer(field, weights, gains, region):
    levels, rows, cols, width = field.shape
    heads = width // HEAD
    hidden_width = (weights.shape[1] - 4 * width) // 2
    count = levels * rows * cols
    bands = rows // WIN_H
    strips = cols // WIN_W
    flat = field.reshape(count, width)
    normed = layer_norm(flat, gains[0]).astype(jnp.bfloat16)
    qkv_all = jnp.dot(normed, weights[:, :3 * width], preferred_element_type=jnp.float32).astype(jnp.bfloat16)
    packed = qkv_all.reshape(levels, bands, WIN_H, strips, WIN_W, 3, heads, HEAD)
    packed = packed.transpose(1, 3, 5, 6, 0, 2, 4, 7).reshape(bands, strips, 3, heads, levels * WIN_H * WIN_W, HEAD)
    query = packed[:, :, 0].astype(jnp.float32)
    keys = packed[:, :, 1].astype(jnp.float32)
    values = packed[:, :, 2].astype(jnp.float32)
    scores = jnp.einsum('bchqe,bchke->bchqk', query, keys) * HEAD ** (-0.5)
    token_region = jnp.broadcast_to(region.reshape(bands, 1, WIN_H, 1), (bands, levels, WIN_H, WIN_W)).reshape(bands, -1)
    allowed = token_region[:, None, None, :, None] == token_region[:, None, None, None, :]
    scores = jnp.where(allowed, scores, jnp.float32(-1e+30))
    top = lax.optimization_barrier(jnp.max(scores, axis=-1, keepdims=True))
    expo = jnp.exp(scores - top)
    probs = (expo / lax.optimization_barrier(jnp.sum(expo, axis=-1, keepdims=True))).astype(jnp.bfloat16)
    mixed = jnp.einsum('bchqk,bchke->bchqe', probs.astype(jnp.float32), values).astype(jnp.bfloat16)
    mixed = mixed.reshape(bands, strips, heads, levels, WIN_H, WIN_W, HEAD).transpose(3, 0, 4, 1, 5, 2, 6).reshape(count, width)
    proj_rows = weights[:, 3 * width + hidden_width:4 * width + hidden_width]
    projected = jnp.einsum('te,de->td', mixed.astype(jnp.float32), proj_rows.astype(jnp.float32))
    resid = flat.astype(jnp.float32) + projected
    normed_two = layer_norm(resid, gains[1]).astype(jnp.bfloat16)
    upward = jnp.dot(normed_two, weights[:, 3 * width:3 * width + hidden_width], preferred_element_type=jnp.float32)
    hidden = jax.nn.gelu(upward, approximate=False).astype(jnp.bfloat16)
    down_rows = weights[:, 4 * width + hidden_width:]
    downward = jnp.einsum('tf,df->td', hidden.astype(jnp.float32), down_rows.astype(jnp.float32))
    return (resid + downward).astype(jnp.bfloat16).reshape(field.shape)

def apply_bands(field, weights, gains, region):
    levels, rows, cols, width = field.shape
    bands = rows // WIN_H
    banded = field.reshape(levels, bands, WIN_H, cols, width).transpose(1, 0, 2, 3, 4)
    band_region = region.reshape(bands, WIN_H)

    def one_band(pair):
        return window_layer(pair[0], weights, gains, pair[1])
    outputs = lax.map(one_band, (banded, band_region))
    return outputs.transpose(1, 0, 2, 3, 4).reshape(field.shape)

def reference(field, weights, gains):
    rows = field.shape[1]
    row_index = jnp.arange(rows, dtype=jnp.int32)
    flat_region = jnp.zeros((rows,), jnp.int32)
    pole_region = jnp.where(row_index < rows - WIN_H, 0, jnp.where(row_index < rows - SHIFT_H, 1, 2)).astype(jnp.int32)
    first = apply_bands(field, weights[0], gains[0], flat_region)
    shifted = jnp.roll(first, (-SHIFT_H, -SHIFT_W), (1, 2))
    second = apply_bands(shifted, weights[1], gains[1], pole_region)
    return jnp.roll(second, (SHIFT_H, SHIFT_W), (1, 2))
```

```python
import functools

import jax
import jax.numpy as jnp
import numpy as np
from jax import lax
from jax.experimental import pallas as pl
from jax.experimental.pallas import tpu as pltpu
from jax.sharding import PartitionSpec as P

F32, BF16 = jnp.float32, jnp.bfloat16
MESH = pl.DeviceIdType.MESH
NT = (((1,), (1,)), ((), ()))
TN = (((0,), (0,)), ((), ()))
NN = (((1,), (0,)), ((), ()))
T = 144
COUNT = 864
WIDTH = 512
STEPS = 6
SLAB = {(0, 0): 0, (1, 0): 32, (0, 1): 64, (1, 1): 96}
START = {(0, 0): 0, (1, 0): 36, (0, 1): 72, (1, 1): 108}
PLACE0 = {(0, 0): 0, (0, 1): 1, (1, 0): 2, (2, 0): 3, (1, 1): 4, (2, 1): 5}
PLACE1 = {(2, 0): 0, (2, 1): 1, (0, 1): 2, (1, 1): 3, (0, 0): 4, (1, 0): 5}


def place_matrices():
    into = np.zeros((288, 288), np.float32)
    out = np.zeros((288, 384), np.float32)
    shift = np.zeros((144, 192), np.float32)
    slabs = [(1, 1), (1, 0), (0, 1), (0, 0)]
    for j in range(2):
        for a in range(2):
            for b in range(2):
                for lev in range(2):
                    for r in range(3):
                        for c in range(6):
                            inner = lev * 18 + r * 6 + c
                            grid = lev * 144 + (a * 3 + r) * 24 + j * 12 + b * 6 + c
                            into[j * 144 + START[a, b] + inner, grid] = 1
                            source = (1 - a, 1 - b)
                            k = slabs.index(source) * 48 + START[source] - SLAB[source] + inner
                            out[grid, j * 192 + k] = 1
                            shift[START[a, b] + inner, k] = 1
    return into, shift, out


def device(x, y, z, c):
    return (lax.rem(x, 2) * 4 + y, (x // 2) * 16 + z * 2 + c)


def norm(v, gain):
    center = v - jnp.mean(v, axis=-1, keepdims=True)
    spread = jnp.mean(center * center, axis=-1, keepdims=True)
    return (center * lax.rsqrt(spread + 1e-5) * gain).astype(BF16)


def gelu(u):
    return 0.5 * u * (1.0 + lax.erf(u * np.float32(0.5**0.5)))


def kernel(
    x_ref, w_ref, g_ref, into_ref, shift_ref, out_ref, o_ref,
    W, X, N, QKV, ATT, R, H, Y, BIAS, HE, HS, HD, BW, BN, BD,
    send_z, send_x, send_y, send_c, recv_zx, recv_zy, recv_x, recv_y, recv_c, halo_send, halo_recv,
):
    lat, lon = lax.axis_index("lat"), lax.axis_index("lon")
    xlo, y = lat // 4, lax.rem(lat, 4)
    xhi, z, c = lon // 16, lax.rem(lon // 2, 8), lax.rem(lon, 2)
    x = xhi * 2 + xlo
    xn = 3 - x
    mine = xhi * 8 + z
    north = (lax.rem(lat + 7, 8), lon)
    south = (lax.rem(lat + 1, 8), lon)
    west = (lat, lax.rem(lon + 31, 32))
    east = (lat, lax.rem(lon + 1, 32))
    nw = (north[0], west[1])
    se = (south[0], east[1])
    sibling = device(x, y, z, 1 - c)
    ring_z = [device(x, y, lax.rem(z + d, 8), c) for d in range(1, 8)]
    cross_z = [device(xn, y, lax.rem(z + d, 8), c) for d in range(8)]
    peers_x = [device(lax.rem(x + d, 4), y, z, c) for d in range(1, 4)]
    peers_y = [device(x, lax.rem(y + d, 4), z, c) for d in range(1, 4)]
    halo = [west, north, nw, east, south, se]

    partners = [sibling] + ring_z + cross_z + peers_x + peers_y + halo
    barrier = pltpu.get_barrier_semaphore()
    for p in partners:
        pl.semaphore_signal(barrier, inc=1, device_id=p, device_id_type=MESH)

    xcols = pl.ds(pl.multiple_of(xlo * 512, 128), 512)
    ycols = pl.ds(pl.multiple_of(1024 + y * 256, 128), 256)
    for b in range(2):
        for f, from_x, from_y in (
            (3 * b, xlo * 512, 1024 + y * 256 + (y // 2) * 2048),
            (3 * b + 1, 1536 + xlo * 512, 2560 + y * 256),
            (3 * b + 2, 4096 + xlo * 512, 5120 + y * 256),
        ):
            W[f, mine, c, :, xcols] = w_ref[b, :, pl.ds(pl.multiple_of(from_x, 128), 512)]
            W[f, mine, c, :, ycols] = w_ref[b, :, pl.ds(pl.multiple_of(from_y, 128), 256)]
    pl.semaphore_wait(barrier, len(partners))

    xrows = pl.ds(xhi * 8, 8)

    def send(ref, s, r, to):
        pltpu.make_async_remote_copy(
            src_ref=ref, dst_ref=ref, send_sem=s, recv_sem=r, device_id=to, device_id_type=MESH
        ).start()

    def arrived(ref, s, r):
        pltpu.make_async_remote_copy(
            src_ref=ref, dst_ref=ref, send_sem=s, recv_sem=r, device_id=sibling, device_id_type=MESH
        ).wait_recv()

    def left(ref, s, r):
        pltpu.make_async_remote_copy(
            src_ref=ref, dst_ref=ref, send_sem=s, recv_sem=r, device_id=sibling, device_id_type=MESH
        ).wait_send()

    def s1(f):
        for to in ring_z:
            send(W.at[f, mine, c, :, xcols], send_z.at[f, 0], recv_zx.at[f], to)
        for to in ring_z + cross_z:
            send(W.at[f, mine, c, :, ycols], send_z.at[f, 1], recv_zy.at[f], to)

    def s2(f):
        arrived(W.at[f, 0:7, 0, :, 0:512], send_z.at[f, 0], recv_zx.at[f])
        for to in peers_x:
            send(W.at[f, xrows, c, :, xcols], send_x.at[f], recv_x.at[f], to)
        arrived(W.at[f, 0:15, 0, :, 0:256], send_z.at[f, 1], recv_zy.at[f])
        for to in peers_y:
            send(W.at[f, :, c, :, ycols], send_y.at[f], recv_y.at[f], to)

    def s3(f):
        arrived(W.at[f, 0:8, 0, :, 0:1536], send_x.at[f], recv_x.at[f])
        arrived(W.at[f, :, 0, :, 0:768], send_y.at[f], recv_y.at[f])
        send(W.at[f, :, c], send_c.at[f], recv_c.at[f], sibling)

    def s4(f):
        arrived(W.at[f, :, 0], send_c.at[f], recv_c.at[f])

    def drain(f):
        left(W.at[f, 0:7, 0, :, 0:512], send_z.at[f, 0], recv_zx.at[f])
        left(W.at[f, 0:15, 0, :, 0:256], send_z.at[f, 1], recv_zy.at[f])
        left(W.at[f, 0:8, 0, :, 0:1536], send_x.at[f], recv_x.at[f])
        left(W.at[f, :, 0, :, 0:768], send_y.at[f], recv_y.at[f])
        left(W.at[f, :, 0], send_c.at[f], recv_c.at[f])

    def weight(f, lo, n):
        return W[f, :, :, :, lo : lo + n].reshape(512, n)

    def rows_of(i, n):
        return pl.ds(pl.multiple_of(i * n, 16), n)

    def enter():
        for i in range(3):
            both = jnp.concatenate(
                [x_ref[144 * i : 144 * i + 144, :], x_ref[432 + 144 * i : 576 + 144 * i, :]], axis=0
            )
            tokens = lax.dot_general(into_ref[...], both, NN, preferred_element_type=F32)
            normed = norm(tokens, g_ref[0:1, :])
            for j in range(2):
                at = PLACE0[i, j] * T
                X[at : at + T, :] = tokens[j * T : j * T + T].astype(BF16)
                N[at : at + T, :] = normed[j * T : j * T + T]

    def project_in(f):
        def body(g, carry):
            rows = rows_of(g, 288)
            for k in range(3):
                part = jnp.dot(N[rows, :], weight(f, 512 * k, 512), preferred_element_type=F32)
                QKV[rows, 512 * k : 512 * k + 512] = part.astype(BF16)
            return carry

        lax.fori_loop(0, 3, body, 0)

    def attend(first, last, masked):
        low = lax.broadcasted_iota(jnp.int32, (T, 128), 1) < 64

        def body(w, carry):
            rows = rows_of(w, T)
            for p in range(4):
                q = QKV[rows, 128 * p : 128 * p + 128] * BF16(0.125)
                k = QKV[rows, 512 + 128 * p : 640 + 128 * p]
                v = QKV[rows, 1024 + 128 * p : 1152 + 128 * p]
                zero = jnp.zeros_like(q)
                pair = jnp.concatenate([jnp.where(low, q, zero), jnp.where(low, zero, q)], axis=0)
                s = lax.dot_general(k, pair, NT, preferred_element_type=F32)
                if masked:
                    s = s + BIAS[...]
                e = jnp.exp(s - jnp.max(s, axis=0, keepdims=True))
                probs = (e * (1.0 / jnp.sum(e, axis=0, keepdims=True))).astype(BF16)
                out = lax.dot_general(probs, v, TN, preferred_element_type=F32)
                ATT[rows, 128 * p : 128 * p + 128] = jnp.where(low, out[:T], out[T:]).astype(BF16)
            return carry

        lax.fori_loop(first, last, body, 0)

    def project_out(f, gain):
        def body(g, carry):
            rows = rows_of(g, 288)
            r = X[rows, :].astype(F32) + lax.dot_general(
                ATT[rows, :], weight(f, 1536, 512), NT, preferred_element_type=F32
            )
            R[rows, :] = r
            N[rows, :] = norm(r, g_ref[gain : gain + 1, :])
            return carry

        lax.fori_loop(0, 3, body, 0)

    def up(f):
        def body(g, carry):
            rows = rows_of(g, 288)
            for k in range(4):
                u = jnp.dot(N[rows, :], weight(f, 512 * k, 512), preferred_element_type=F32)
                H[rows, 512 * k : 512 * k + 512] = gelu(u).astype(BF16)
            return carry

        lax.fori_loop(0, 3, body, 0)

    def down(f, first, last):
        def body(g, carry):
            rows = rows_of(g, 288)
            total = R[rows, :]
            for k in range(4):
                total = total + lax.dot_general(
                    H[rows, 512 * k : 512 * k + 512], weight(f, 512 * k, 512), NT, preferred_element_type=F32
                )
            Y[rows, :] = total.astype(BF16)
            return carry

        lax.fori_loop(first, last, body, 0)

    def halo_pairs(forward):
        def y_rows(place, w, a, b):
            return Y.at[place[w] * T + a : place[w] * T + b, :]

        if forward:
            p = PLACE0
            return [
                (y_rows(p, (0, 0), 64, 112), HS.at[0, 64:112, :], north),
                (y_rows(p, (0, 1), 0, 112), HS.at[1, 0:112, :], north),
                (y_rows(p, (0, 0), 0, 48), HD.at[0:48, :], nw),
                (y_rows(p, (0, 0), 32, 80), HE.at[0, 32:80, :], west),
                (y_rows(p, (1, 0), 0, 80), HE.at[1, 0:80, :], west),
                (y_rows(p, (2, 0), 0, 80), HE.at[2, 0:80, :], west),
            ]
        p = PLACE1
        return [
            (y_rows(p, (2, 0), 32, 144), BN.at[0, 32:144, :], south),
            (y_rows(p, (2, 1), 32, 80), BN.at[1, 32:80, :], south),
            (y_rows(p, (2, 1), 96, 144), BD.at[96:144, :], se),
            (y_rows(p, (2, 1), 64, 112), BW.at[2, 64:112, :], east),
            (y_rows(p, (0, 1), 64, 144), BW.at[0, 64:144, :], east),
            (y_rows(p, (1, 1), 64, 144), BW.at[1, 64:144, :], east),
        ]

    def halo_copies(forward):
        base = 0 if forward else 6
        return [
            pltpu.make_async_remote_copy(
                src_ref=src, dst_ref=dst, send_sem=halo_send.at[base + i], recv_sem=halo_recv.at[base + i],
                device_id=to, device_id_type=MESH,
            )
            for i, (src, dst, to) in enumerate(halo_pairs(forward))
        ]

    def quarter(place, w, q):
        at = place[w] * T + SLAB[q]
        return Y[at : at + 48, :]

    def shift_windows(gain):
        def take(i, j, q):
            lo = SLAB[q]
            if i < 3 and j < 2:
                return quarter(PLACE0, (i, j), q)
            if i < 3:
                return HE[i, lo : lo + 48, :]
            if j < 2:
                return HS[j, lo : lo + 48, :]
            return HD[lo : lo + 48, :]

        for (i, j), at in PLACE1.items():
            parts = jnp.concatenate(
                [take(i, j, (1, 1)), take(i, j + 1, (1, 0)), take(i + 1, j, (0, 1)), take(i + 1, j + 1, (0, 0))],
                axis=0,
            )
            tokens = lax.dot_general(shift_ref[...], parts, NN, preferred_element_type=F32)
            X[at * T : at * T + T, :] = tokens.astype(BF16)
            N[at * T : at * T + T, :] = norm(tokens, g_ref[gain : gain + 1, :])

    def leave():
        def take(i, j, q):
            lo = SLAB[q]
            if i >= 0 and j >= 0:
                return quarter(PLACE1, (i, j), q)
            if i >= 0:
                return BW[i, lo : lo + 48, :]
            if j >= 0:
                return BN[j, lo : lo + 48, :]
            return BD[lo : lo + 48, :]

        for i in (2, 1, 0):
            parts = []
            for j in range(2):
                parts += [
                    take(i - 1, j - 1, (1, 1)), take(i - 1, j, (1, 0)), take(i, j - 1, (0, 1)), take(i, j, (0, 0)),
                ]
            tokens = lax.dot_general(
                out_ref[...], jnp.concatenate(parts, axis=0), NN, preferred_element_type=F32
            ).astype(BF16)
            o_ref[144 * i : 144 * i + 144, :] = tokens[:144]
            o_ref[432 + 144 * i : 576 + 144 * i, :] = tokens[144:]

    s1(0)
    s1(1)
    enter()
    key = lax.broadcasted_iota(jnp.int32, (T, 288), 0)
    query = lax.broadcasted_iota(jnp.int32, (T, 288), 1)
    query = jnp.where(query < T, query, query - T)

    def lower(t):
        return ((t >= 36) & (t < 72)) | (t >= 108)

    differ = jnp.where(lower(key), 1, 0) != jnp.where(lower(query), 1, 0)
    BIAS[...] = jnp.where(differ, jnp.where(lat == 7, jnp.float32(-1e30), jnp.float32(0)), jnp.float32(0))

    s2(0)
    s1(2)
    s2(1)
    s1(3)
    s3(0)
    s2(2)
    s4(0)
    project_in(0)
    s3(1)
    attend(0, 3, False)
    s1(4)
    s2(3)
    attend(3, 6, False)
    s3(2)
    project_out(0, 1)
    s4(1)
    s1(5)
    up(1)
    s2(4)
    s3(3)
    s4(2)
    there = halo_copies(True)
    down(2, 0, 1)
    for cp in there[:4]:
        cp.start()
    down(2, 1, 2)
    for cp in there[4:]:
        cp.start()
    down(2, 2, 3)
    s2(5)
    for cp in there:
        cp.wait_recv()
    shift_windows(2)
    s3(4)
    s4(3)
    project_in(3)
    attend(0, 2, True)
    s3(5)
    attend(2, 6, False)
    project_out(3, 3)
    s4(4)
    up(4)
    for cp in there:
        cp.wait_send()
    s4(5)
    back = halo_copies(False)
    down(5, 0, 1)
    for cp in back[:4]:
        cp.start()
    down(5, 1, 2)
    for cp in back[4:]:
        cp.start()
    down(5, 2, 3)
    for f in range(STEPS):
        drain(f)
    for cp in back:
        cp.wait_recv()
    leave()
    for cp in back:
        cp.wait_send()


def on_device(field, weights, gains):
    into, shift, out = (jnp.asarray(m, BF16) for m in place_matrices())
    vmem = pl.BlockSpec(memory_space=pltpu.VMEM)
    dma = pltpu.SemaphoreType.DMA
    result = pl.pallas_call(
        kernel,
        out_shape=jax.ShapeDtypeStruct((COUNT, WIDTH), BF16),
        in_specs=[vmem] * 6,
        out_specs=vmem,
        scratch_shapes=[
            pltpu.VMEM((STEPS, 16, 2, 16, 2048), BF16),
            pltpu.VMEM((COUNT, WIDTH), BF16),
            pltpu.VMEM((COUNT, WIDTH), BF16),
            pltpu.VMEM((COUNT, 3 * WIDTH), BF16),
            pltpu.VMEM((COUNT, WIDTH), BF16),
            pltpu.VMEM((COUNT, WIDTH), F32),
            pltpu.VMEM((COUNT, 4 * WIDTH), BF16),
            pltpu.VMEM((COUNT, WIDTH), BF16),
            pltpu.VMEM((T, 288), F32),
            pltpu.VMEM((3, T, WIDTH), BF16),
            pltpu.VMEM((2, T, WIDTH), BF16),
            pltpu.VMEM((T, WIDTH), BF16),
            pltpu.VMEM((3, T, WIDTH), BF16),
            pltpu.VMEM((2, T, WIDTH), BF16),
            pltpu.VMEM((T, WIDTH), BF16),
            dma((STEPS, 2)),
            dma((STEPS,)),
            dma((STEPS,)),
            dma((STEPS,)),
            dma((STEPS,)),
            dma((STEPS,)),
            dma((STEPS,)),
            dma((STEPS,)),
            dma((STEPS,)),
            dma((12,)),
            dma((12,)),
        ],
        compiler_params=pltpu.CompilerParams(
            collective_id=0, has_side_effects=True, vmem_limit_bytes=48 * 2**20
        ),
    )(field.reshape(COUNT, WIDTH), weights, gains.reshape(4, WIDTH), into, shift, out)
    return result.reshape(field.shape)


def solution(mesh):
    return jax.shard_map(
        on_device,
        mesh=mesh,
        in_specs=(P(None, "lat", "lon", None), P(None, "lon", None), P()),
        out_specs=P(None, "lat", "lon", None),
        check_vma=False,
    )
```

```python
import functools

import jax
import jax.numpy as jnp
import numpy as np
from jax import lax
from jax.experimental import pallas as pl
from jax.experimental.pallas import tpu as pltpu
from jax.sharding import PartitionSpec as P

F32, BF16 = jnp.float32, jnp.bfloat16
MESH = pl.DeviceIdType.MESH
NT = (((1,), (1,)), ((), ()))
TN = (((0,), (0,)), ((), ()))
NN = (((1,), (0,)), ((), ()))
UNROLL = 2
T = 144
COUNT = 864
WIDTH = 512
PHASES = [
    (0, 0, 512, 1024, 1, 1),
    (0, 3072, 512, 512, 1, 1),
    (0, 1536, 1024, 512, 1, 1),
    (0, 4096, 1024, 1024, 1, 1),
    (1, 0, 512, 1024, 1, 1),
    (1, 1536, 1536, 1024, 1, 1),
    (1, 4096, 512, 512, 1, 1),
    (1, 5120, 512, 512, 1, 1),
]
STEPS = len(PHASES)
Z_TWO = [p[4] for p in PHASES]
XY_TWO = [p[5] for p in PHASES]
KINDS = ("zx", "zy", "fx", "fy", "x", "y", "gx", "gy", "cx", "cy")
SLAB = {(0, 0): 0, (1, 0): 32, (0, 1): 64, (1, 1): 96}
START = {(0, 0): 0, (1, 0): 36, (0, 1): 72, (1, 1): 108}
PLACE0 = {(0, 0): 0, (0, 1): 1, (1, 0): 2, (2, 0): 3, (1, 1): 4, (2, 1): 5}
PLACE1 = {(0, 1): 0, (1, 1): 1, (2, 0): 2, (2, 1): 3, (0, 0): 4, (1, 0): 5}


def place_matrices():
    into = np.zeros((288, 288), np.float32)
    shift = np.zeros((144, 192), np.float32)
    slabs = [(1, 1), (1, 0), (0, 1), (0, 0)]
    for j in range(2):
        for a in range(2):
            for b in range(2):
                for lev in range(2):
                    for r in range(3):
                        for c in range(6):
                            inner = lev * 18 + r * 6 + c
                            grid = lev * 144 + (a * 3 + r) * 24 + j * 12 + b * 6 + c
                            into[j * 144 + START[a, b] + inner, grid] = 1
                            source = (1 - a, 1 - b)
                            k = slabs.index(source) * 48 + START[source] - SLAB[source] + inner
                            shift[START[a, b] + inner, k] = 1
    return into, shift, into.T


def device(x, y, z, c):
    return (lax.rem(x, 2) * 4 + y, (x // 2) * 16 + z * 2 + c)


def norm(v, gain):
    center = v - jnp.mean(v, axis=-1, keepdims=True)
    spread = jnp.mean(center * center, axis=-1, keepdims=True)
    return (center * lax.rsqrt(spread + 1e-5) * gain).astype(BF16)


def gelu(u):
    return 0.5 * u * (1.0 + lax.erf(u * np.float32(0.5**0.5)))


def kernel(
    x_ref, w_ref, g_hbm, into_hbm, shift_hbm, out_hbm, o_ref,
    *refs
):
    WX, WY = refs[:STEPS], refs[STEPS : 2 * STEPS]
    (
    X, N, QKV, ATT, R, H, Y, BIAS, HE, HS, HD, BW, BN, BD,
    g_ref, into_ref, shift_ref, out_ref, local, send_sem, recv_sem, halo_send, halo_recv,
    ) = refs[2 * STEPS :]
    lat, lon = lax.axis_index("lat"), lax.axis_index("lon")
    xlo, y = lat // 4, lax.rem(lat, 4)
    xhi, z, c = lon // 16, lax.rem(lon // 2, 8), lax.rem(lon, 2)
    x = xhi * 2 + xlo
    xn = 3 - x
    north = (lax.rem(lat + 7, 8), lon)
    south = (lax.rem(lat + 1, 8), lon)
    west = (lat, lax.rem(lon + 31, 32))
    east = (lat, lax.rem(lon + 1, 32))
    nw = (north[0], west[1])
    se = (south[0], east[1])
    sibling = device(x, y, z, 1 - c)
    ring_z = [device(x, y, lax.rem(z + d, 8), c) for d in range(8)]
    cross_z = [device(xn, y, lax.rem(z + d, 8), c) for d in range(8)]
    peers_x = [device(lax.rem(x + d, 4), y, z, c) for d in range(4)]
    peers_y = [device(x, lax.rem(y + d, 4), z, c) for d in range(4)]
    halo = [west, north, nw, east, south, se]

    partners = [sibling] + ring_z[1:] + cross_z + peers_x[1:] + peers_y[1:] + halo
    barrier = pltpu.get_barrier_semaphore()
    for p in partners:
        pl.semaphore_signal(barrier, inc=1, device_id=p, device_id_type=MESH)

    def half_of(f, chip_x, x_hi, shards):
        return WX[f].at[lax.rem(chip_x, 2), c, x_hi, shards]

    def quarter_of(f, chip_y, x_hi, shards):
        return WY[f].at[chip_y, c, x_hi, shards]

    def own_rows(f):
        b, first, n, m = PHASES[f][:4]
        from_x = first + xlo * (n // 2)
        from_y = first + n + y * (m // 4)
        return [
            pltpu.make_async_copy(
                w_ref.at[b, :, pl.ds(pl.multiple_of(from_x, 128), n // 2)],
                half_of(f, x, xhi, z), local.at[2 * f],
            ),
            pltpu.make_async_copy(
                w_ref.at[b, :, pl.ds(pl.multiple_of(from_y, 128), m // 4)],
                quarter_of(f, y, xhi, z), local.at[2 * f + 1],
            ),
        ]

    own = [own_rows(f) for f in range(STEPS)]
    others = [
        pltpu.make_async_copy(src, dst, local.at[2 * STEPS + i])
        for i, (src, dst) in enumerate(
            [(x_ref, Y), (into_hbm, into_ref), (g_hbm, g_ref), (shift_hbm, shift_ref), (out_hbm, out_ref)]
        )
    ]
    for cp in own[0] + others[:3] + sum(own[1:], []) + others[3:]:
        cp.start()
    for cp in own[0]:
        cp.wait()
    pl.semaphore_wait(barrier, len(partners))

    def copy(f, kind, ref, to):
        k = KINDS.index(kind)
        return pltpu.make_async_remote_copy(
            src_ref=ref, dst_ref=ref, send_sem=send_sem.at[f, k], recv_sem=recv_sem.at[f, k],
            device_id=to, device_id_type=MESH,
        )

    def total(f, kind):
        far, two = 1 - Z_TWO[f], XY_TWO[f]
        h, q = WX[f], WY[f]
        return {
            "zx": h.at[0, 0, 0, 0 : 7 if far else 4],
            "zy": q.at[0:3, 0, 0, 0 : 5 if far else 3],
            "fx": h.at[0, 0, 0, 0:3],
            "fy": q.at[0, 0, :, 0:3],
            "x": h.at[0, 0] if two else h.at[0, :, :, 0:6],
            "y": q.at[0 : 2 if two else 3, 0],
            "gx": h.at[0, 0, 0],
            "gy": q.at[0, 0],
            "cx": h.at[:, 0],
            "cy": q.at[:, 0],
        }[kind]

    def arrived(f, *kinds):
        for kind in kinds:
            copy(f, kind, total(f, kind), sibling).wait_recv()

    def z_near(f):
        if f:
            for cp in own[f]:
                cp.wait()
        ways = (1, 7, 2, 6) if Z_TWO[f] else (1, 7, 2, 6, 3, 5, 4)
        cross = (0, 1, 7, 2, 6) if Z_TWO[f] else (0, 1, 7, 2, 6, 3, 5, 4)
        mine_x = half_of(f, x, xhi, z)
        mine_y = quarter_of(f, y, xhi, z)
        for d in ways:
            copy(f, "zx", mine_x, ring_z[d]).start()
        for d in ways:
            copy(f, "zy", mine_y, ring_z[d]).start()
        for d in cross:
            copy(f, "zy", mine_y, cross_z[d]).start()

    def z_far(f):
        arrived(f, "zx", "zy")
        below, above = lax.rem(z + 6, 8), lax.rem(z + 2, 8)
        for shard, d in ((below, 1), (above, 7), (below, 2)):
            copy(f, "fx", half_of(f, x, xhi, shard), ring_z[d]).start()
        for shard, d in ((below, 1), (above, 7), (above, 6)):
            copy(f, "fy", quarter_of(f, y, slice(None), shard), ring_z[d]).start()

    def xy_near(f):
        arrived(f, *(("fx", "fy") if Z_TWO[f] else ("zx", "zy")))
        for d in (1, 3) if XY_TWO[f] else (1, 3, 2):
            copy(f, "x", half_of(f, x, xhi, slice(None)), peers_x[d]).start()
        for d in (1, 3) if XY_TWO[f] else (1, 3, 2):
            copy(f, "y", quarter_of(f, y, slice(None), slice(None)), peers_y[d]).start()

    def xy_far(f):
        arrived(f, "x", "y")
        below, above = lax.rem(x + 3, 4), lax.rem(x + 1, 4)
        copy(f, "gx", half_of(f, below, below // 2, slice(0, 4)), peers_x[1]).start()
        copy(f, "gx", half_of(f, above, above // 2, slice(4, 8)), peers_x[3]).start()
        below, above = lax.rem(y + 3, 4), lax.rem(y + 1, 4)
        copy(f, "gy", quarter_of(f, below, 0, slice(None)), peers_y[1]).start()
        copy(f, "gy", quarter_of(f, above, 1, slice(None)), peers_y[3]).start()

    def share(f):
        arrived(f, *(("gx", "gy") if XY_TWO[f] else ("x", "y")))
        copy(f, "cx", WX[f].at[:, c], sibling).start()
        copy(f, "cy", WY[f].at[:, c], sibling).start()

    def ready(f):
        arrived(f, "cx", "cy")

    def drain(f):
        kinds = ("zx", "zy", "x", "y", "cx", "cy") + ("fx", "fy") * Z_TWO[f] + ("gx", "gy") * XY_TWO[f]
        for kind in kinds:
            copy(f, kind, total(f, kind), sibling).wait_send()

    def weight(block, lo, n):
        f = [
            i for i, p in enumerate(PHASES) if p[0] == block and p[1] <= lo and lo + n <= p[1] + p[2] + p[3]
        ][0]
        lo -= PHASES[f][1]
        parts = []
        while n:
            if lo < PHASES[f][2]:
                ref, size, at = WX[f], PHASES[f][2] // 2, lo
            else:
                ref, size, at = WY[f], PHASES[f][3] // 4, lo - PHASES[f][2]
            begin = at % size
            take = min(n, size - begin)
            cores = [ref[at // size, k, :, :, :, begin : begin + take] for k in range(2)]
            parts.append(jnp.stack(cores, axis=2).reshape(512, take))
            lo, n = lo + take, n - take
        return parts[0] if len(parts) == 1 else jnp.concatenate(parts, axis=1)

    def loop(n, body, hooks, first=0):
        def step(g, carry):
            for i, hook in hooks.items():
                pl.when(g == i)(hook)
            body(g)
            return carry

        lax.fori_loop(first, n, step, 0)

    def rows_of(i, n):
        return pl.ds(pl.multiple_of(i * n, 16), n)

    def enter():
        for i in range(3):
            both = jnp.concatenate(
                [Y[144 * i : 144 * i + 144, :], Y[432 + 144 * i : 576 + 144 * i, :]], axis=0
            )
            tokens = lax.dot_general(into_ref[...], both, NN, preferred_element_type=F32)
            normed = norm(tokens, g_ref[0, 0:1, :])
            for j in range(2):
                at = PLACE0[i, j] * T
                X[at : at + T, :] = tokens[j * T : j * T + T].astype(BF16)
                N[at : at + T, :] = normed[j * T : j * T + T]

    def project_in(block, k):
        for n in range(512 * k, 512 * k + 512, 256):
            QKV[:, n : n + 256] = jnp.dot(N[...], weight(block, n, 256), preferred_element_type=F32).astype(BF16)

    def attend(block, hooks):
        low = lax.broadcasted_iota(jnp.int32, (T, 128), 1) < 64

        def body(g):
            for w in range(3):
                for p in range(4):
                    rows = rows_of(3 * g + w, T)
                    at = 128 * p
                    q = QKV[rows, at : at + 128] * BF16(0.125)
                    k = QKV[rows, at + 512 : at + 640]
                    v = QKV[rows, at + 1024 : at + 1152]
                    zero = jnp.zeros_like(q)
                    pair = jnp.concatenate([jnp.where(low, q, zero), jnp.where(low, zero, q)], axis=0)
                    s = lax.dot_general(k, pair, NT, preferred_element_type=F32)
                    if block and w != 1:
                        s = s + BIAS[g if w == 0 else 1 - g]
                    e = jnp.exp(s - jnp.max(s, axis=0, keepdims=True))
                    probs = (e * (1.0 / jnp.sum(e, axis=0, keepdims=True))).astype(BF16)
                    out = lax.dot_general(probs, v, TN, preferred_element_type=F32)
                    ATT[rows, at : at + 128] = jnp.where(low, out[:T], out[T:]).astype(BF16)

        loop(2, body, hooks)

    def project_out(block, hooks):
        def body(g):
            rows = rows_of(g, 432)
            base, attended = (Y[rows, :], QKV[rows, 0:512]) if block else (X[rows, :], ATT[rows, :])
            r = base.astype(F32) + lax.dot_general(
                attended, weight(block, 3584, 512), NT, preferred_element_type=F32
            )
            R[rows, :] = r
            N[rows, :] = norm(r, g_ref[block, 1:2, :])

        loop(2, body, hooks)

    def up(block, k):
        for n in range(512 * k, 512 * k + 512, 256):
            u = jnp.dot(N[...], weight(block, 1536 + n, 256), preferred_element_type=F32)
            H[:, n : n + 256] = gelu(u).astype(BF16)

    def down(block, k, hooks):
        def body(g):
            rows = rows_of(g, 288)
            acc = R[rows, :] + lax.dot_general(
                H[rows, 1024 * k : 1024 * k + 1024], weight(block, 4096 + 1024 * k, 1024), NT,
                preferred_element_type=F32,
            )
            if k and block:
                X[rows, :] = acc.astype(BF16)
            elif k:
                Y[rows, :] = acc.astype(BF16)
            else:
                R[rows, :] = acc

        loop(3, body, hooks)

    def halo_pairs(forward):
        def y_rows(place, w, a, b):
            return (Y if forward else ATT).at[place[w] * T + a : place[w] * T + b, :]

        if forward:
            p = PLACE0
            return [
                (y_rows(p, (0, 0), 64, 112), HS.at[0, 64:112, :], north),
                (y_rows(p, (0, 1), 0, 112), HS.at[1, 0:112, :], north),
                (y_rows(p, (0, 0), 0, 48), HD.at[0:48, :], nw),
                (y_rows(p, (0, 0), 32, 80), HE.at[0, 32:80, :], west),
                (y_rows(p, (1, 0), 0, 80), HE.at[1, 0:80, :], west),
                (y_rows(p, (2, 0), 0, 80), HE.at[2, 0:80, :], west),
            ]
        p = PLACE1
        return [
            (y_rows(p, (0, 1), 64, 144), BW.at[0, 64:144, :], east),
            (y_rows(p, (1, 1), 64, 144), BW.at[1, 64:144, :], east),
            (y_rows(p, (2, 1), 64, 112), BW.at[2, 64:112, :], east),
            (y_rows(p, (2, 0), 32, 144), BN.at[0, 32:144, :], south),
            (y_rows(p, (2, 1), 32, 80), BN.at[1, 32:80, :], south),
            (y_rows(p, (2, 1), 96, 144), BD.at[96:144, :], se),
        ]

    def halo_copies(forward):
        base = 0 if forward else 6
        return [
            pltpu.make_async_remote_copy(
                src_ref=src, dst_ref=dst, send_sem=halo_send.at[base + i], recv_sem=halo_recv.at[base + i],
                device_id=to, device_id_type=MESH,
            )
            for i, (src, dst, to) in enumerate(halo_pairs(forward))
        ]

    def quarter(ref, place, w, q):
        at = place[w] * T + SLAB[q]
        return ref[at : at + 48, :]

    def shift_windows():
        def take(i, j, q):
            lo = SLAB[q]
            if i < 3 and j < 2:
                return quarter(Y, PLACE0, (i, j), q)
            if i < 3:
                return HE[i, lo : lo + 48, :]
            if j < 2:
                return HS[j, lo : lo + 48, :]
            return HD[lo : lo + 48, :]

        for (i, j), at in PLACE1.items():
            parts = jnp.concatenate(
                [take(i, j, (1, 1)), take(i, j + 1, (1, 0)), take(i + 1, j, (0, 1)), take(i + 1, j + 1, (0, 0))],
                axis=0,
            )
            tokens = lax.dot_general(shift_ref[...], parts, NN, preferred_element_type=F32)
            N[at * T : at * T + T, :] = norm(tokens, g_ref[1, 0:1, :])

    def unshift():
        def take(i, j, q):
            lo = SLAB[q]
            if i >= 0 and j >= 0:
                return quarter(ATT, PLACE1, (i, j), q)
            if i >= 0:
                return BW[i, lo : lo + 48, :]
            if j >= 0:
                return BN[j, lo : lo + 48, :]
            return BD[lo : lo + 48, :]

        for (i, j), at in PLACE0.items():
            parts = [take(i - 1, j - 1, (1, 1)), take(i - 1, j, (1, 0)), take(i, j - 1, (0, 1)), take(i, j, (0, 0))]
            rows = lax.dot_general(
                shift_ref[...], jnp.concatenate(parts, axis=0), NN, preferred_element_type=F32
            )
            QKV[at * T : at * T + T, 0:512] = rows.astype(BF16)

    def leave():
        for i in range(3):
            pair = [X[PLACE0[i, j] * T : PLACE0[i, j] * T + T, :] for j in range(2)]
            tokens = lax.dot_general(
                out_ref[...], jnp.concatenate(pair, axis=0), NN, preferred_element_type=F32
            ).astype(BF16)
            o_ref[144 * i : 144 * i + 144, :] = tokens[:144]
            o_ref[432 + 144 * i : 576 + 144 * i, :] = tokens[144:]

    z_near(0)
    z_near(1)
    z_near(2)
    for cp in others:
        cp.wait()
    enter()
    z_near(3)
    key = lax.broadcasted_iota(jnp.int32, (T, 288), 0)
    query = lax.broadcasted_iota(jnp.int32, (T, 288), 1)
    query = jnp.where(query < T, query, query - T)

    def lower(t):
        return ((t >= 36) & (t < 72)) | (t >= 108)

    differ = jnp.where(lower(key), 1, 0) != jnp.where(lower(query), 1, 0)
    BIAS[0] = jnp.zeros((T, 288), F32)
    BIAS[1] = jnp.where(differ, jnp.where(lat == 7, jnp.float32(-1e30), jnp.float32(0)), jnp.float32(0))
    z_far(0)
    z_far(1)
    z_near(4)
    z_far(2)
    z_far(3)
    xy_near(0)
    z_near(5)
    xy_near(1)
    z_far(4)
    xy_near(2)
    z_near(6)
    xy_far(0)
    xy_near(3)
    z_near(7)
    xy_far(1)
    z_far(5)
    xy_far(2)
    xy_near(4)
    share(0)
    z_far(6)
    z_far(7)
    ready(0)
    project_in(0, 0)
    project_in(0, 1)
    xy_far(3)
    project_in(0, 2)
    share(1)
    xy_near(5)
    xy_near(6)

    def hook0():
        ready(1)
        share(2)
        xy_near(7)

    attend(0, {1: hook0})
    xy_far(4)

    def hook1():
        ready(2)
        share(3)

    project_out(0, {1: hook1})
    up(0, 3)
    up(0, 0)
    up(0, 1)
    up(0, 2)
    ready(3)

    def hook2():
        xy_far(5)

    down(0, 0, {2: hook2})
    there = halo_copies(True)

    def hook3():
        for cp in there[:4]:
            cp.start()
        xy_far(6)


    def hook4():
        for cp in there[4:]:
            cp.start()

    down(0, 1, {1: hook3, 2: hook4})
    xy_far(7)
    share(4)
    for cp in there:
        cp.wait_recv()
    shift_windows()
    share(5)
    ready(4)
    project_in(1, 0)
    share(6)
    project_in(1, 1)
    project_in(1, 2)
    share(7)
    back = halo_copies(False)

    def hook5():
        for k in (3, 0, 1):
            back[k].start()
        ready(5)

    attend(1, {1: hook5})
    for k in (4, 5, 2):
        back[k].start()
    ready(6)
    ready(7)
    for cp in back:
        cp.wait_recv()
    unshift()
    project_out(1, {})
    up(1, 3)
    up(1, 0)
    up(1, 1)
    up(1, 2)
    down(1, 0, {})
    down(1, 1, {})
    leave()
    for f in range(STEPS):
        drain(f)
    for cp in there + back:
        cp.wait_send()


def on_device(field, weights, gains):
    into, shift, out = (jnp.asarray(m, BF16) for m in place_matrices())
    dma = pltpu.SemaphoreType.DMA
    tokens = [pltpu.VMEM((COUNT, n), t) for n, t in (
        (512, BF16), (512, BF16), (1536, BF16), (512, BF16), (512, F32), (2048, BF16), (512, BF16)
    )]
    halos = [pltpu.VMEM(n + (T, WIDTH), BF16) for n in ((3,), (2,), (), (3,), (2,), ())]
    result = pl.pallas_call(
        kernel,
        out_shape=jax.ShapeDtypeStruct((COUNT, WIDTH), BF16),
        in_specs=[pl.BlockSpec(memory_space=pl.ANY)] * 6,
        out_specs=pl.BlockSpec(memory_space=pltpu.VMEM),
        scratch_shapes=[pltpu.VMEM((2, 2, 2, 8, 16, p[2] // 2), BF16) for p in PHASES]
        + [pltpu.VMEM((4, 2, 2, 8, 16, p[3] // 4), BF16) for p in PHASES]
        + tokens
        + [pltpu.VMEM((2, T, 288), F32)]
        + halos
        + [
            pltpu.VMEM((2, 2, WIDTH), F32),
            pltpu.VMEM((288, 288), BF16),
            pltpu.VMEM((T, 192), BF16),
            pltpu.VMEM((288, 288), BF16),
            dma((2 * STEPS + 5,)),
            dma((STEPS, len(KINDS))),
            dma((STEPS, len(KINDS))),
            dma((12,)),
            dma((12,)),
        ],
        compiler_params=pltpu.CompilerParams(
            collective_id=0, has_side_effects=True, vmem_limit_bytes=56 * 2**20
        ),
    )(field.reshape(COUNT, WIDTH), weights, gains, into, shift, out)
    return result.reshape(field.shape)


def solution(mesh):
    return jax.shard_map(
        on_device,
        mesh=mesh,
        in_specs=(P(None, "lat", "lon", None), P(None, "lon", None), P()),
        out_specs=P(None, "lat", "lon", None),
        check_vma=False,
    )
```
